32 devices in a mesh: strip: 32 (over z, y, x, core).
Axes of the slice: x: 2, y: 2, z: 4, core: 2. Of those that a mesh axis runs over, the one named last changes fastest.
Arguments:
- params: float32 [59, 163840], P(None, 'strip'), may hold values from -23 to 23, as said below
- camera: float32 [4, 12], replicated, may hold values from -2 to 2, as said below
- send_index: int32 [1024, 320], P('strip'), may hold values from 0 to 5119, as said below
- send_count: int32 [1024], P('strip'), may hold values from 0 to 320, as said below
- tile_list: int32 [1280, 128], P('strip'), may hold values from 0 to 5119, as said below
- target: float32 [3, 512, 640], P(None, 'strip'), may hold values from 0 to 1
Outputs:
- param_grads: float32 [59, 163840], P(None, 'strip')
The draws below stay inside these ranges and needn't reach their ends.
Inputs may be any that keep to these rules, and one draw needn't show every extreme that they name: `send_index`: in row s * 32 + r the first send_count[s * 32 + r] entries are distinct local Gaussian numbers of device s; over all r these live entries name each of device s's 5120 Gaussians exactly once. Later entries are local Gaussian numbers that name nothing sent. `send_count`: for every sender, and for every strip, the counts sum to 5120; the largest count equals 320. `tile_list`: each row holds 128 distinct received numbers of its strip; every number 0 to 5119 of a strip stands in exactly one of the strip's lists. `params`: each Gaussian lies 2 to 6 in front of the camera of the view of the strip that receives it and projects inside the tile whose list holds it; entry 6 of every Gaussian is 1 or more. `camera`: the first nine entries of each row form a rotation matrix.
All inputs are finite; a program needn't handle non-finite values.
Results may differ from the reference program's by a relative error of at most 0.0003.
Values sent between devices are 32-bit elements; how exact they have to be, the bound alone decides.
A program may use at most 64 MiB of HBM per device.

```python
import math
import jax
import jax.numpy as jnp
from jax import lax

TILE_ROWS = 1
IMG_W = 640
VIEWS = 4
LIST = 128
PARAMS = 59
TILES_DEV = 40
G_DEV = 5120
CAP = 320
GAUSS = 163840
TILES = 1280
ROWS = 512
VIEW_ROWS = 128
N_STRIP = 32


def camera_table(key):
    first, second = jax.random.split(jax.random.fold_in(key, 202))
    raw = jax.random.uniform(first, (VIEWS, 4), jnp.float32, -1.0, 1.0)
    raw = raw.at[:, 0].add(2.0)
    versor = raw / jnp.sqrt(jnp.sum(raw * raw, axis=1, keepdims=True))
    real, imag_x, imag_y, imag_z = (versor[:, 0], versor[:, 1], versor[:, 2], versor[:, 3])
    rows = jnp.stack([1.0 - 2.0 * (imag_y * imag_y + imag_z * imag_z), 2.0 * (imag_x * imag_y - real * imag_z), 2.0 * (imag_x * imag_z + real * imag_y), 2.0 * (imag_x * imag_y + real * imag_z), 1.0 - 2.0 * (imag_x * imag_x + imag_z * imag_z), 2.0 * (imag_y * imag_z - real * imag_x), 2.0 * (imag_x * imag_z - real * imag_y), 2.0 * (imag_y * imag_z + real * imag_x), 1.0 - 2.0 * (imag_x * imag_x + imag_y * imag_y)], axis=1)
    shift = jax.random.uniform(second, (VIEWS, 3), jnp.float32, -1.0, 1.0)
    return jnp.concatenate([rows, shift], axis=1)


def routing(key):
    strips = N_STRIP
    mean_load = G_DEV // strips
    quarter = mean_load // 4
    keys = jax.random.split(jax.random.fold_in(key, 101), 6)

    def wave(subkey):
        heights = jax.random.randint(subkey, (strips,), -quarter, quarter + 1, dtype=jnp.int32)
        heights = heights.at[0].set(quarter).at[1].set(-quarter)
        return heights - jnp.roll(heights, -1)
    rise = wave(keys[0])
    fall = wave(keys[1])
    source = jnp.arange(strips, dtype=jnp.int32)[:, None]
    dest_strip = jnp.arange(strips, dtype=jnp.int32)[None, :]
    base = mean_load + rise[(dest_strip - source) % strips] + fall[(dest_strip + source) % strips]
    row_order = jax.random.permutation(keys[2], strips)
    col_order = jax.random.permutation(keys[3], strips)
    loads = base[row_order][:, col_order].astype(jnp.int32)
    orders = jax.vmap(lambda subkey: jax.random.permutation(subkey, G_DEV))(jax.random.split(keys[4], strips)).astype(jnp.int32)
    starts = jnp.cumsum(loads, axis=1) - loads
    slot = jnp.arange(CAP, dtype=jnp.int32)
    position = (starts[:, :, None] + slot[None, None, :]) % G_DEV
    sends = jax.vmap(lambda order, place: order[place])(orders, position)
    inverse = jax.vmap(lambda order: jnp.zeros((G_DEV,), jnp.int32).at[order].set(jnp.arange(G_DEV, dtype=jnp.int32)))(orders)
    ends = starts + loads
    dest = jax.vmap(lambda edge, place: jnp.searchsorted(edge, place, side='right'))(ends, inverse).astype(jnp.int32)
    within = inverse - jnp.take_along_axis(starts, dest, axis=1)
    in_starts = jnp.cumsum(loads, axis=0) - loads
    compact = jnp.take_along_axis(in_starts, dest, axis=1) + within
    arrange = jax.vmap(lambda subkey: jax.random.permutation(subkey, G_DEV))(jax.random.split(keys[5], strips)).astype(jnp.int32)
    place_of = jax.vmap(lambda order: jnp.zeros((G_DEV,), jnp.int32).at[order].set(jnp.arange(G_DEV, dtype=jnp.int32)))(arrange)
    tile = place_of[dest, compact] // LIST
    return (loads, sends, arrange, dest, tile)


def draw_send_index(key, part):
    return routing(key)[1].reshape(N_STRIP * N_STRIP, CAP)


def draw_send_count(key, part):
    return routing(key)[0].reshape(N_STRIP * N_STRIP)


def draw_tile_list(key, part):
    return routing(key)[2].reshape(TILES, LIST)


def draw_camera(key, part):
    return camera_table(key)


def draw_params(key, part):
    loads, sends, arrange, dest, tile = routing(key)
    camera = camera_table(key)
    per_view = N_STRIP // VIEWS
    tile_cols = IMG_W // 16
    noise = jax.random.split(jax.random.fold_in(key, 303), 8)
    shape = (N_STRIP, G_DEV)
    logical = (dest + per_view // 2) % N_STRIP
    view = logical // per_view
    pixel_x = (tile % tile_cols * 16).astype(jnp.float32) + jax.random.uniform(noise[0], shape, jnp.float32, 2.0, 14.0)
    pixel_y = ((logical % per_view * TILE_ROWS + tile // tile_cols) * 16).astype(jnp.float32) + jax.random.uniform(noise[1], shape, jnp.float32, 2.0, 14.0)
    depth = jax.random.uniform(noise[2], shape, jnp.float32, 2.0, 6.0)
    focal = 0.5 * IMG_W
    placed = [(pixel_x - 0.5 * IMG_W) / focal * depth, (pixel_y - 0.5 * VIEW_ROWS) / focal * depth, depth]
    rows = camera[view]
    relative = [placed[axis] - rows[:, :, 9 + axis] for axis in range(3)]
    mean = [rows[:, :, col] * relative[0] + rows[:, :, 3 + col] * relative[1] + rows[:, :, 6 + col] * relative[2] for col in range(3)]
    sigma = jax.random.uniform(noise[3], (3,) + shape, jnp.float32, 1.5, 4.0)
    logit = jax.random.uniform(noise[4], shape, jnp.float32, -5.0, -1.5)
    first_band = jax.random.uniform(noise[5], (3,) + shape, jnp.float32, -1.0, 1.0)
    higher = jax.random.uniform(noise[6], (45,) + shape, jnp.float32, -0.4, 0.4)
    log_scale = jnp.log(sigma * depth[None] / focal)
    quaternion = jax.random.uniform(noise[7], (4,) + shape, jnp.float32, -1.0, 1.0)
    quaternion = quaternion.at[0].set(jnp.abs(quaternion[0]) + 1.0)
    stacked = jnp.concatenate([jnp.stack(mean), log_scale, quaternion, logit[None], first_band, higher], axis=0)
    return stacked.reshape(PARAMS, GAUSS).astype(jnp.float32)


def shard_levels(key, dims, cuts, smallest, high):
    factor_of = 1.0
    for dim, parts in cuts:
        steps = jax.random.uniform(jax.random.fold_in(jax.random.fold_in(key, 6), dim), (parts,), jnp.float32, smallest / len(cuts), high / len(cuts))
        factor_of = factor_of * jnp.repeat(jnp.exp(steps), dims[dim] // parts).reshape((-1,) + (1,) * (len(dims) - 1 - dim))
    return factor_of


def setup_inputs(seed: int = 0) -> dict:
    seeds = jax.random.split(jax.random.key(seed), 7)
    params = draw_params(jax.random.fold_in(seeds[6], 71), 0)
    camera = draw_camera(jax.random.fold_in(seeds[6], 71), 0)
    send_index = draw_send_index(jax.random.fold_in(seeds[6], 71), 0)
    send_count = draw_send_count(jax.random.fold_in(seeds[6], 71), 0)
    tile_list = draw_tile_list(jax.random.fold_in(seeds[6], 71), 0)
    target = jnp.clip(1.0 * jax.random.uniform(seeds[5], (3, ROWS, IMG_W), jnp.float32) ** shard_levels(seeds[5], (3, ROWS, IMG_W), ((1, 32),), -0.2, 0.2), 0.0, 1.0)
    return {"params": params, "camera": camera, "send_index": send_index, "send_count": send_count, "tile_list": tile_list, "target": target}


exact_dot = lax.Precision.HIGHEST
harmonic_zero = 0.28209479177387814
harmonic_one = 0.4886025119029199
harmonic_two = (1.0925484305920792, -1.0925484305920792, 0.31539156525252005, -1.0925484305920792, 0.5462742152960396)
harmonic_three = (-0.5900435899266435, 2.890611442640554, -0.4570457994644658, 0.3731763325901154, -0.4570457994644658, 1.445305721320277, -0.5900435899266435)
light_term = 0.0001
contrast_term = 0.0009

def harmonics(along_x, along_y, along_z):
    square_x = along_x * along_x
    square_y = along_y * along_y
    square_z = along_z * along_z
    return [harmonic_zero + 0.0 * along_x, -harmonic_one * along_y, harmonic_one * along_z, -harmonic_one * along_x, harmonic_two[0] * along_x * along_y, harmonic_two[1] * along_y * along_z, harmonic_two[2] * (2.0 * square_z - square_x - square_y), harmonic_two[3] * along_x * along_z, harmonic_two[4] * (square_x - square_y), harmonic_three[0] * along_y * (3.0 * square_x - square_y), harmonic_three[1] * along_x * along_y * along_z, harmonic_three[2] * along_y * (4.0 * square_z - square_x - square_y), harmonic_three[3] * along_z * (2.0 * square_z - 3.0 * square_x - 3.0 * square_y), harmonic_three[4] * along_x * (4.0 * square_z - square_x - square_y), harmonic_three[5] * along_z * (square_x - square_y), harmonic_three[6] * along_x * (square_x - 3.0 * square_y)]

def project(params, camera, focal, centre_x, centre_y, alive):
    rotation = [[camera[3 * row + col] for col in range(3)] for row in range(3)]
    mean = [params[axis] for axis in range(3)]
    placed = [rotation[row][0] * mean[0] + rotation[row][1] * mean[1] + rotation[row][2] * mean[2] + camera[9 + row] for row in range(3)]
    depth = placed[2]
    if alive is not None:
        depth = jnp.where(alive, depth, 1.0)
    inverse = 1.0 / depth
    screen_x = focal * placed[0] * inverse + centre_x
    screen_y = focal * placed[1] * inverse + centre_y
    quaternion = params[6:10]
    versor = quaternion * lax.rsqrt(lax.optimization_barrier(jnp.sum(quaternion * quaternion, axis=0)))
    real, imag_x, imag_y, imag_z = (versor[0], versor[1], versor[2], versor[3])
    turn = [[1.0 - 2.0 * (imag_y * imag_y + imag_z * imag_z), 2.0 * (imag_x * imag_y - real * imag_z), 2.0 * (imag_x * imag_z + real * imag_y)], [2.0 * (imag_x * imag_y + real * imag_z), 1.0 - 2.0 * (imag_x * imag_x + imag_z * imag_z), 2.0 * (imag_y * imag_z - real * imag_x)], [2.0 * (imag_x * imag_z - real * imag_y), 2.0 * (imag_y * imag_z + real * imag_x), 1.0 - 2.0 * (imag_x * imag_x + imag_y * imag_y)]]
    scales = jnp.exp(params[3:6])
    jacobian = [[focal * inverse, 0.0 * inverse, -focal * placed[0] * inverse * inverse], [0.0 * inverse, focal * inverse, -focal * placed[1] * inverse * inverse]]
    facing = [[jacobian[row][0] * rotation[0][col] + jacobian[row][1] * rotation[1][col] + jacobian[row][2] * rotation[2][col] for col in range(3)] for row in range(2)]
    stretch = [[(facing[row][0] * turn[0][col] + facing[row][1] * turn[1][col] + facing[row][2] * turn[2][col]) * scales[col] for col in range(3)] for row in range(2)]
    cov_xx = stretch[0][0] * stretch[0][0] + stretch[0][1] * stretch[0][1] + stretch[0][2] * stretch[0][2] + 0.3
    cov_xy = stretch[0][0] * stretch[1][0] + stretch[0][1] * stretch[1][1] + stretch[0][2] * stretch[1][2]
    cov_yy = stretch[1][0] * stretch[1][0] + stretch[1][1] * stretch[1][1] + stretch[1][2] * stretch[1][2] + 0.3
    determinant = cov_xx * cov_yy - cov_xy * cov_xy
    safe = [placed[0], placed[1], depth]
    length = jnp.sqrt(safe[0] * safe[0] + safe[1] * safe[1] + safe[2] * safe[2])
    heading = [(rotation[0][col] * safe[0] + rotation[1][col] * safe[1] + rotation[2][col] * safe[2]) / length for col in range(3)]
    basis = jnp.stack(harmonics(heading[0], heading[1], heading[2]))
    coefficients = params[11:59].reshape(16, 3, -1)
    colour = 0.5 + lax.optimization_barrier(jnp.sum(basis[:, None, :] * coefficients, axis=0))
    opacity = jax.nn.sigmoid(params[10])
    return jnp.stack([screen_x, screen_y, cov_yy / determinant, -cov_xy / determinant, cov_xx / determinant, colour[0], colour[1], colour[2], opacity])

def blend_tiles(footprint, anchor_x, anchor_y):
    pixel = jnp.arange(256, dtype=jnp.int32)
    inside_x = (pixel % 16).astype(jnp.float32) + 0.5
    inside_y = (pixel // 16).astype(jnp.float32) + 0.5
    apart_x = anchor_x[:, None, None] + inside_x[None, :, None] - footprint[0][:, None, :]
    apart_y = anchor_y[:, None, None] + inside_y[None, :, None] - footprint[1][:, None, :]
    power = -0.5 * (footprint[2][:, None, :] * apart_x * apart_x + footprint[4][:, None, :] * apart_y * apart_y) - footprint[3][:, None, :] * apart_x * apart_y
    alpha = footprint[8][:, None, :] * jnp.exp(power)
    passed = jnp.log1p(-alpha)
    before = jnp.cumsum(passed, axis=2) - passed
    weight = alpha * jnp.exp(before)
    return jnp.einsum('tpl,ctl->ctp', weight, footprint[5:8], precision=exact_dot)

def window_weights():
    offsets = jnp.arange(11, dtype=jnp.float32) - 5.0
    raw = jnp.exp(-offsets * offsets / 4.5)
    return raw / jnp.sum(raw)

def smooth(field, weights, out_rows):
    width = field.shape[2]
    total = weights[0] * field[:, 0:out_rows, :]
    for shift in range(1, 11):
        total = total + weights[shift] * field[:, shift:shift + out_rows, :]
    padded = jnp.pad(total, ((0, 0), (0, 0), (5, 5)))
    result = weights[0] * padded[:, :, 0:width]
    for shift in range(1, 11):
        result = result + weights[shift] * padded[:, :, shift:shift + width]
    return result

def similarity(mean_x, mean_y, power_x, power_y, cross):
    var_x = power_x - mean_x * mean_x
    var_y = power_y - mean_y * mean_y
    covar = cross - mean_x * mean_y
    upper = (2.0 * mean_x * mean_y + light_term) * (2.0 * covar + contrast_term)
    lower = (mean_x * mean_x + mean_y * mean_y + light_term) * (var_x + var_y + contrast_term)
    return upper / lower

def pad_rows(field):
    return jnp.pad(field, ((0, 0), (5, 5), (0, 0)))

def reference(params, camera, send_index, send_count, tile_list, target):
    strips = N_STRIP
    per_view = strips // VIEWS
    offset = per_view // 2
    width = IMG_W
    focal = 0.5 * width
    counts = send_count.reshape(strips, strips)
    sends = send_index.reshape(strips, strips, CAP)
    lists = tile_list.reshape(strips, TILES_DEV * LIST)
    tile_cols = width // 16
    tile_num = jnp.arange(TILES_DEV, dtype=jnp.int32)
    anchor_x = (tile_num % tile_cols * 16).astype(jnp.float32)
    block = math.gcd(16, TILES_DEV)
    groups = TILES_DEV // block
    weights = window_weights()

    def render_strip(values, strip):
        counts_in = counts[:, strip]
        keys = lists[strip]
        ends = jnp.cumsum(counts_in)
        before = ends[None, :] <= keys[:, None]
        source = lax.optimization_barrier(jnp.sum(before.astype(jnp.int32), axis=1))
        start = lax.optimization_barrier(jnp.sum(jnp.where(before, counts_in[None, :], 0), axis=1))
        local = sends[source, strip, keys - start]
        entries = values[:, source * G_DEV + local]
        position = (strip + offset) % strips
        camera_row = lax.dynamic_index_in_dim(camera, position // per_view, 0, keepdims=False)[:, None]
        footprint = project(entries, camera_row, focal, 0.5 * width, 0.5 * VIEW_ROWS, None)
        anchor_y = ((position % per_view * TILE_ROWS + tile_num // tile_cols) * 16).astype(jnp.float32)
        feet = footprint.reshape(9, groups, block, LIST).transpose(1, 0, 2, 3)
        colours = lax.map(lambda item: jax.checkpoint(blend_tiles)(item[0], item[1], item[2]), (feet, anchor_x.reshape(groups, block), anchor_y.reshape(groups, block)))
        flat = colours.transpose(1, 0, 2, 3).reshape(3, TILE_ROWS, tile_cols, 16, 16)
        return flat.transpose(0, 1, 3, 2, 4).reshape(3, 16 * TILE_ROWS, width)

    def total_loss(values):
        images = lax.map(lambda strip: jax.checkpoint(render_strip)(values, strip), jnp.arange(strips, dtype=jnp.int32))
        images = jnp.roll(images, offset, axis=0)
        rendered = images.transpose(1, 0, 2, 3).reshape(3 * VIEWS, VIEW_ROWS, width)
        seen = jnp.roll(target, offset * 16 * TILE_ROWS, axis=1).reshape(3 * VIEWS, VIEW_ROWS, width)
        whole = pad_rows(rendered)
        truth = pad_rows(seen)
        score = similarity(smooth(whole, weights, VIEW_ROWS), smooth(truth, weights, VIEW_ROWS), smooth(whole * whole, weights, VIEW_ROWS), smooth(truth * truth, weights, VIEW_ROWS), smooth(whole * truth, weights, VIEW_ROWS))
        return jnp.sum(1.0 - score)
    return jax.grad(total_loss)(params)
```

```python
import functools
import math

import jax
import jax.numpy as jnp
import numpy as np
from jax import lax
from jax.experimental import pallas as pl
from jax.experimental.pallas import tpu as pltpu
from jax.sharding import PartitionSpec as P

VIEWS = 4
FEET = 9
LANES = 128
LOG2E = math.log2(math.e)
NT = (((1,), (1,)), ((), ()))

exact_dot = lax.Precision.HIGHEST
harmonic_zero = 0.28209479177387814
harmonic_one = 0.4886025119029199
harmonic_two = (
    1.0925484305920792,
    -1.0925484305920792,
    0.31539156525252005,
    -1.0925484305920792,
    0.5462742152960396,
)
harmonic_three = (
    -0.5900435899266435,
    2.890611442640554,
    -0.4570457994644658,
    0.3731763325901154,
    -0.4570457994644658,
    1.445305721320277,
    -0.5900435899266435,
)
light_term = 0.0001
contrast_term = 0.0009


def harmonics(along_x, along_y, along_z):
    square_x = along_x * along_x
    square_y = along_y * along_y
    square_z = along_z * along_z
    return [
        harmonic_zero + 0.0 * along_x,
        -harmonic_one * along_y,
        harmonic_one * along_z,
        -harmonic_one * along_x,
        harmonic_two[0] * along_x * along_y,
        harmonic_two[1] * along_y * along_z,
        harmonic_two[2] * (2.0 * square_z - square_x - square_y),
        harmonic_two[3] * along_x * along_z,
        harmonic_two[4] * (square_x - square_y),
        harmonic_three[0] * along_y * (3.0 * square_x - square_y),
        harmonic_three[1] * along_x * along_y * along_z,
        harmonic_three[2] * along_y * (4.0 * square_z - square_x - square_y),
        harmonic_three[3] * along_z * (2.0 * square_z - 3.0 * square_x - 3.0 * square_y),
        harmonic_three[4] * along_x * (4.0 * square_z - square_x - square_y),
        harmonic_three[5] * along_z * (square_x - square_y),
        harmonic_three[6] * along_x * (square_x - 3.0 * square_y),
    ]


def project(params, camera, focal, centre_x, centre_y):
    rotation = [[camera[3 * row + col] for col in range(3)] for row in range(3)]
    mean = [params[axis] for axis in range(3)]
    placed = [
        rotation[row][0] * mean[0]
        + rotation[row][1] * mean[1]
        + rotation[row][2] * mean[2]
        + camera[9 + row]
        for row in range(3)
    ]
    depth = placed[2]
    inverse = 1.0 / depth
    screen_x = focal * placed[0] * inverse + centre_x
    screen_y = focal * placed[1] * inverse + centre_y
    quaternion = params[6:10]
    shrink = lax.rsqrt(sum(part * part for part in quaternion))
    real, imag_x, imag_y, imag_z = [part * shrink for part in quaternion]
    turn = [
        [
            1.0 - 2.0 * (imag_y * imag_y + imag_z * imag_z),
            2.0 * (imag_x * imag_y - real * imag_z),
            2.0 * (imag_x * imag_z + real * imag_y),
        ],
        [
            2.0 * (imag_x * imag_y + real * imag_z),
            1.0 - 2.0 * (imag_x * imag_x + imag_z * imag_z),
            2.0 * (imag_y * imag_z - real * imag_x),
        ],
        [
            2.0 * (imag_x * imag_z - real * imag_y),
            2.0 * (imag_y * imag_z + real * imag_x),
            1.0 - 2.0 * (imag_x * imag_x + imag_y * imag_y),
        ],
    ]
    scales = [jnp.exp(part) for part in params[3:6]]
    jacobian = [
        [focal * inverse, None, -focal * placed[0] * inverse * inverse],
        [None, focal * inverse, -focal * placed[1] * inverse * inverse],
    ]
    facing = [
        [
            jacobian[row][row] * rotation[row][col]
            + jacobian[row][2] * rotation[2][col]
            for col in range(3)
        ]
        for row in range(2)
    ]
    stretch = [
        [
            (
                facing[row][0] * turn[0][col]
                + facing[row][1] * turn[1][col]
                + facing[row][2] * turn[2][col]
            )
            * scales[col]
            for col in range(3)
        ]
        for row in range(2)
    ]
    cov_xx = (
        stretch[0][0] * stretch[0][0]
        + stretch[0][1] * stretch[0][1]
        + stretch[0][2] * stretch[0][2]
        + 0.3
    )
    cov_xy = (
        stretch[0][0] * stretch[1][0]
        + stretch[0][1] * stretch[1][1]
        + stretch[0][2] * stretch[1][2]
    )
    cov_yy = (
        stretch[1][0] * stretch[1][0]
        + stretch[1][1] * stretch[1][1]
        + stretch[1][2] * stretch[1][2]
        + 0.3
    )
    determinant = cov_xx * cov_yy - cov_xy * cov_xy
    safe = [placed[0], placed[1], depth]
    length = jnp.sqrt(safe[0] * safe[0] + safe[1] * safe[1] + safe[2] * safe[2])
    heading = [
        (rotation[0][col] * safe[0] + rotation[1][col] * safe[1] + rotation[2][col] * safe[2])
        / length
        for col in range(3)
    ]
    basis = harmonics(heading[0], heading[1], heading[2])
    colour = [
        0.5 + sum(basis[k] * params[11 + 3 * k + channel] for k in range(16)) for channel in range(3)
    ]
    log_opacity = -jnp.log1p(jnp.exp(-params[10]))
    return [
        screen_x,
        screen_y,
        cov_yy / determinant,
        -cov_xy / determinant,
        cov_xx / determinant,
        colour[0],
        colour[1],
        colour[2],
        log_opacity,
    ]


def similarity(mean_x, mean_y, power_x, power_y, cross):
    var_x = power_x - mean_x * mean_x
    var_y = power_y - mean_y * mean_y
    covar = cross - mean_x * mean_y
    upper = (2.0 * mean_x * mean_y + light_term) * (2.0 * covar + contrast_term)
    lower = (mean_x * mean_x + mean_y * mean_y + light_term) * (var_x + var_y + contrast_term)
    return upper / lower


def iota(shape, dim):
    return lax.broadcasted_iota(jnp.int32, shape, dim)


def split_three(values):
    high = values.astype(jnp.bfloat16)
    rest = values - high.astype(jnp.float32)
    middle = rest.astype(jnp.bfloat16)
    low = (rest - middle.astype(jnp.float32)).astype(jnp.bfloat16)
    return high, middle, low


def split_two(values):
    high = values.astype(jnp.bfloat16)
    return high, (values - high.astype(jnp.float32)).astype(jnp.bfloat16)


def one_hot(row, size, dtype=jnp.float32):
    hit = iota((size, row.shape[1]), 0) == row
    return jnp.where(hit, 1.0, 0.0).astype(dtype)


def pick_camera(view, camera_ref):
    picked = []
    for entry in range(12):
        value = jnp.full(view.shape, camera_ref[0, entry], jnp.float32)
        for number in range(1, VIEWS):
            value = jnp.where(view == float(number), camera_ref[number, entry], value)
        picked.append(value)
    return picked


def owner_kernel(
    geometry, offset, per_view, params_ref, camera_ref, index_ref, count_ref,
    message_ref, view_ref, low_ref, owner_ref
):
    strips = message_ref.shape[0]
    blocks = params_ref.shape[1]
    slots = index_ref.shape[1]
    span = slots // strips
    parts = span // LANES

    @pl.loop(0, strips)
    def _(strip):
        here = pl.ds(pl.multiple_of(strip * span, LANES), span)
        index = index_ref[:, here]
        low_ref[:, here] = one_hot(index & 127, LANES, jnp.bfloat16)
        view = (lax.rem(strip + offset, strips) // per_view).astype(jnp.float32)
        live = iota((1, span), 1) < count_ref[strip]
        mark = jnp.where(live, view, 0.0)
        owner_ref[:, here] = one_hot(index >> 7, blocks) * mark

    view = lax.dot_general(
        owner_ref[...].astype(jnp.bfloat16), low_ref[...], NT, preferred_element_type=jnp.float32
    )
    view_ref[...] = view
    camera = pick_camera(view, camera_ref)
    feet = project([params_ref[entry] for entry in range(59)], camera, *geometry)
    packed = jnp.concatenate(split_three(jnp.concatenate(feet, axis=0)), axis=1)

    @pl.loop(0, strips)
    def _(strip):
        here = pl.ds(pl.multiple_of(strip * span, LANES), span)
        low = low_ref[:, here]
        found = jnp.dot(
            packed, jnp.concatenate([low, low, low], axis=0), preferred_element_type=jnp.float32
        )
        high = one_hot(index_ref[:, here] >> 7, blocks)
        chosen = jnp.sum(found.reshape(FEET, blocks, span) * high[None], axis=1)
        for part in range(parts):
            message_ref[strip, part * FEET : (part + 1) * FEET, :] = chosen[
                :, part * LANES : (part + 1) * LANES
            ]
        message_ref[strip, parts * FEET : parts * FEET + 1, :] = jnp.full(
            (1, LANES), count_ref[strip].astype(jnp.float32)
        )


def source_hits(starts, ends, keys):
    return jnp.where((keys >= starts) & (keys < ends), 1.0, 0.0)


def blend_kernel(
    parts, tiles, chunk, arrived_ref, keys_ref, anchor_ref, powers_ref,
    rendered_ref, feet_ref, place_ref, alpha_ref, pass_ref, columns_ref, packed_ref
):
    strips, rows, _ = arrived_ref.shape
    total = keys_ref.shape[1]
    counts = arrived_ref[:, parts * FEET, :]
    order = iota((strips, strips), 0) >= iota((strips, strips), 1)
    ends = jnp.dot(
        jnp.where(order, 1.0, 0.0), counts, precision=exact_dot, preferred_element_type=jnp.float32
    )
    starts = ends - counts
    ends = ends[:, 0:1]
    starts = starts[:, 0:1]
    packed_ref[...] = jnp.concatenate(
        split_three(arrived_ref[...].reshape(strips * rows, LANES)), axis=1
    )
    powers = powers_ref[...]

    @pl.loop(0, total // chunk)
    def _(step):
        here = pl.ds(pl.multiple_of(step * chunk, LANES), chunk)
        keys = keys_ref[:, here].astype(jnp.float32)
        hits = source_hits(starts, ends, keys)
        slot = (keys - jnp.sum(hits * starts, axis=0, keepdims=True)).astype(jnp.int32)
        low = one_hot(slot & 127, LANES, jnp.bfloat16)
        found = jnp.dot(
            packed_ref[...],
            jnp.concatenate([low, low, low], axis=0),
            preferred_element_type=jnp.float32,
        )
        chosen = jnp.sum(found.reshape(strips, rows, chunk) * hits[:, None, :], axis=0)
        high = slot >> 7
        feet = chosen[0:FEET]
        for part in range(1, parts):
            feet = jnp.where(high == part, chosen[part * FEET : (part + 1) * FEET], feet)
        source = jnp.sum(hits * iota(hits.shape, 0).astype(jnp.float32), axis=0, keepdims=True)
        place_ref[0:1, here] = source.astype(jnp.int32)
        place_ref[1:2, here] = slot
        row = [feet[entry : entry + 1] for entry in range(FEET)]
        off_x = row[0] - anchor_ref[0:1, here]
        off_y = row[1] - anchor_ref[1:2, here]
        conic_a, conic_b, conic_c = row[2], row[3], row[4]
        feet_ref[:, here] = jnp.concatenate([off_x, off_y, conic_a, conic_b, conic_c], axis=0)
        terms = jnp.concatenate(
            [
                LOG2E
                * (
                    row[8]
                    - 0.5 * (conic_a * off_x * off_x + conic_c * off_y * off_y)
                    - conic_b * off_x * off_y
                ),
                LOG2E * (conic_a * off_x + conic_b * off_y),
                LOG2E * (conic_c * off_y + conic_b * off_x),
                (-0.5 * LOG2E) * conic_a,
                -LOG2E * conic_b,
                (-0.5 * LOG2E) * conic_c,
                jnp.zeros((2, chunk), jnp.float32),
            ],
            axis=0,
        )
        pieces = [piece.astype(jnp.float32) for piece in split_three(terms)]
        colours = jnp.concatenate(row[5:8] + [jnp.zeros((5, chunk), jnp.float32)], axis=0)
        columns = jnp.transpose(jnp.concatenate(pieces + [colours], axis=0))
        columns_ref[here, :] = columns
        power = jnp.dot(columns.astype(jnp.bfloat16), powers, preferred_element_type=jnp.float32)
        alpha_ref[here, :] = jnp.exp2(power)

    def forward(entry, carry):
        clear, red, green, blue = carry
        here = pl.ds(pl.multiple_of(entry * tiles, 8), tiles)
        pass_ref[here, :] = clear
        weight = alpha_ref[here, :] * clear
        tint = columns_ref[here, :]
        return (
            clear - weight,
            red + tint[:, 24:25] * weight,
            green + tint[:, 25:26] * weight,
            blue + tint[:, 26:27] * weight,
        )

    nothing = jnp.zeros((tiles, 256), jnp.float32)
    _, red, green, blue = lax.fori_loop(
        0, total // tiles, forward, (nothing + 1.0, nothing, nothing, nothing), unroll=2
    )
    rendered_ref[0] = red
    rendered_ref[1] = green
    rendered_ref[2] = blue


def loss_kernel(whole_ref, truth_ref, inside_ref, down_ref, back_ref, across_ref, grad_ref):
    rows = grad_ref.shape[1]
    centres = down_ref.shape[0]
    fields = []
    for channel in range(3):
        seen = whole_ref[channel]
        truth = truth_ref[channel]
        fields += [seen, truth, seen * seen, truth * truth, seen * truth]

    def smooth(matrix, items):
        stacked = jnp.concatenate(
            [
                jnp.dot(matrix, item, precision=exact_dot, preferred_element_type=jnp.float32)
                for item in items
            ],
            axis=0,
        )
        return jnp.dot(
            stacked, across_ref[...], precision=exact_dot, preferred_element_type=jnp.float32
        )

    smoothed = smooth(down_ref[...], fields)
    inside = inside_ref[...]
    partials = []
    for channel in range(3):
        mean_x, mean_y, power_x, power_y, cross = [
            smoothed[(5 * channel + item) * centres : (5 * channel + item + 1) * centres]
            for item in range(5)
        ]
        value, pull = jax.vjp(
            lambda first, second, third: similarity(first, mean_y, second, power_y, third),
            mean_x,
            power_x,
            cross,
        )
        partials += [
            jnp.where(inside > 0.0, part, 0.0) for part in pull(jnp.full_like(value, -1.0))
        ]
    spread = smooth(back_ref[...], partials)
    depth = 10
    for channel in range(3):
        first, second, third = [
            spread[(3 * channel + item) * rows : (3 * channel + item + 1) * rows]
            for item in range(3)
        ]
        seen = whole_ref[channel][depth : depth + rows]
        truth = truth_ref[channel][depth : depth + rows]
        grad_ref[channel] = first + 2.0 * seen * second + truth * third


def pull_kernel(
    parts, tiles, chunk, grad_ref, feet_ref, place_ref, alpha_ref, pass_ref, columns_ref,
    moments_ref, message_ref, change_ref, tints_ref
):
    total = feet_ref.shape[1]
    entries = total // tiles
    grads = [grad_ref[channel] for channel in range(3)]
    lane = iota((tiles, LANES), 1)

    def backward(step, behind):
        entry = entries - 1 - step
        here = pl.ds(pl.multiple_of(entry * tiles, 8), tiles)
        alpha = alpha_ref[here, :]
        clear = pass_ref[here, :]
        tint = columns_ref[here, :]
        shade = (
            grads[0] * tint[:, 24:25] + grads[1] * tint[:, 25:26] + grads[2] * tint[:, 26:27]
        )
        excess = shade - behind
        weight = alpha * clear
        change_ref[here, :] = weight * excess
        sums = [jnp.sum(weight * grad, axis=1, keepdims=True) for grad in grads]
        tints_ref[here, :] = jnp.where(
            lane == 0, sums[0], jnp.where(lane == 1, sums[1], jnp.where(lane == 2, sums[2], 0.0))
        )
        return behind + alpha * excess

    lax.fori_loop(
        0, entries, backward, jnp.zeros((tiles, 256), jnp.float32), unroll=2
    )
    message_ref[...] = jnp.zeros_like(message_ref)
    moments = moments_ref[...]
    return moments, total


def scatter_steps(strips, rows, parts, chunk, refs, moments, total):
    feet_ref, place_ref, message_ref, change_ref, tints_ref = refs

    @pl.loop(0, total // chunk)
    def _(step):
        here = pl.ds(pl.multiple_of(step * chunk, LANES), chunk)
        high, low = split_two(change_ref[here, :])
        sums = tints_ref[here, :] + jnp.dot(
            jnp.concatenate([high, low], axis=1), moments, preferred_element_type=jnp.float32
        )
        lines = jnp.transpose(sums)
        plain, by_x, by_y, by_xx, by_xy, by_yy = [lines[item : item + 1] for item in range(3, 9)]
        feet = feet_ref[:, here]
        off_x, off_y, conic_a, conic_b, conic_c = [feet[item : item + 1] for item in range(5)]
        far_x = by_x - off_x * plain
        far_y = by_y - off_y * plain
        far_xx = by_xx - 2.0 * off_x * by_x + off_x * off_x * plain
        far_yy = by_yy - 2.0 * off_y * by_y + off_y * off_y * plain
        far_xy = by_xy - off_x * by_y - off_y * by_x + off_x * off_y * plain
        slopes = jnp.concatenate(
            [
                conic_a * far_x + conic_b * far_y,
                conic_c * far_y + conic_b * far_x,
                -0.5 * far_xx,
                -far_xy,
                -0.5 * far_yy,
                lines[0:3],
                plain,
            ],
            axis=0,
        )
        source = place_ref[0:1, here]
        slot = place_ref[1:2, here]
        part_of = slot >> 7
        laid = [jnp.where(part_of == part, slopes, 0.0) for part in range(parts)]
        laid.append(jnp.zeros((rows - parts * FEET, chunk), jnp.float32))
        laid = jnp.concatenate(laid, axis=0)
        first = laid.astype(jnp.bfloat16).astype(jnp.float32)
        hits = one_hot(source, strips)[:, None, :]
        spread = jnp.concatenate(
            [
                (hits * piece[None]).reshape(strips * rows, chunk).astype(jnp.bfloat16)
                for piece in (first, laid - first)
            ],
            axis=1,
        )
        lows = one_hot(slot & 127, LANES, jnp.bfloat16)
        message_ref[...] += lax.dot_general(
            spread,
            jnp.concatenate([lows, lows], axis=1),
            NT,
            preferred_element_type=jnp.float32,
        )


def return_kernel(
    strips, rows, parts, tiles, chunk, grad_ref, feet_ref, place_ref, alpha_ref, pass_ref,
    columns_ref, moments_ref, message_ref, change_ref, tints_ref
):
    moments, total = pull_kernel(
        parts, tiles, chunk, grad_ref, feet_ref, place_ref, alpha_ref, pass_ref, columns_ref,
        moments_ref, message_ref, change_ref, tints_ref
    )
    refs = (feet_ref, place_ref, message_ref, change_ref, tints_ref)
    scatter_steps(strips, rows, parts, chunk, refs, moments, total)


def gather_kernel(
    geometry, params_ref, camera_ref, index_ref, view_ref, returned_ref, out_ref, sum_ref
):
    strips = returned_ref.shape[0]
    blocks = params_ref.shape[1]
    span = index_ref.shape[1] // strips
    parts = span // LANES
    sum_ref[...] = jnp.zeros_like(sum_ref)

    @pl.loop(0, strips)
    def _(strip):
        here = pl.ds(pl.multiple_of(strip * span, LANES), span)
        index = index_ref[:, here]
        low = one_hot(index & 127, LANES, jnp.bfloat16)
        high = one_hot(index >> 7, blocks)[None]
        block = returned_ref[strip]
        slopes = jnp.concatenate(
            [block[part * FEET : (part + 1) * FEET] for part in range(parts)], axis=1
        )
        first = slopes.astype(jnp.bfloat16).astype(jnp.float32)
        spread = jnp.concatenate(
            [
                (high * piece[:, None, :]).reshape(FEET * blocks, span).astype(jnp.bfloat16)
                for piece in (first, slopes - first)
            ],
            axis=1,
        )
        sum_ref[...] += lax.dot_general(
            spread, jnp.concatenate([low, low], axis=1), NT, preferred_element_type=jnp.float32
        )

    camera = pick_camera(view_ref[...], camera_ref)
    ignored, pull = jax.vjp(
        lambda values: project(values, camera, *geometry),
        [params_ref[entry] for entry in range(59)],
    )
    slopes = [sum_ref[entry * blocks : (entry + 1) * blocks, :] for entry in range(FEET)]
    for entry, slope in enumerate(pull(slopes)[0]):
        out_ref[entry] = slope


def window_weights():
    offsets = np.arange(11, dtype=np.float64) - 5.0
    raw = np.exp(-offsets * offsets / 4.5)
    return raw / raw.sum()


def band(out_rows, out_pad, in_pad, shift):
    weights = window_weights()
    matrix = np.zeros((out_pad, in_pad), np.float32)
    for row in range(out_rows):
        for tap in range(11):
            column = row + tap + shift
            if 0 <= column < in_pad:
                matrix[row, column] = weights[tap]
    return matrix


def pixel_powers():
    pixel = np.arange(256)
    along_x = pixel % 16 - 7.5
    along_y = pixel // 16 - 7.5
    return np.stack(
        [
            np.ones(256),
            along_x,
            along_y,
            along_x * along_x,
            along_x * along_y,
            along_y * along_y,
        ]
    )


def round_up(value, step):
    return -(-value // step) * step


def per_device(params, camera, send_index, send_count, tile_list, target):
    strips = lax.axis_size("strip")
    index = lax.axis_index("strip")
    per_view = strips // VIEWS
    offset = per_view // 2
    position = (index + offset) % strips
    rows_strip = target.shape[1]
    width = target.shape[2]
    view_rows = rows_strip * per_view
    focal = 0.5 * width
    geometry = (focal, 0.5 * width, 0.5 * view_rows)
    tiles, count = tile_list.shape
    total = tiles * count
    chunk = math.gcd(512, total)
    capacity = send_index.shape[1]
    parts = -(-capacity // LANES)
    span = parts * LANES
    rows = round_up(parts * FEET + 1, 16)
    local = params.shape[1]
    blocks = local // LANES
    vmem = pltpu.MemorySpace.VMEM
    smem = pltpu.MemorySpace.SMEM
    big = pltpu.CompilerParams(vmem_limit_bytes=56 * 1024 * 1024)

    def space(*kinds):
        return [pl.BlockSpec(memory_space=kind) for kind in kinds]

    def shaped(*shape, dtype=jnp.float32):
        return jax.ShapeDtypeStruct(shape, dtype)

    params_cut = params.reshape(59, blocks, LANES)
    slot_index = jnp.pad(send_index, ((0, 0), (0, span - capacity))).reshape(1, strips * span)
    message, view = pl.pallas_call(
        functools.partial(owner_kernel, geometry, offset, per_view),
        out_shape=(shaped(strips, rows, LANES), shaped(blocks, LANES)),
        in_specs=space(vmem, smem, vmem, smem),
        out_specs=tuple(space(vmem, vmem)),
        scratch_shapes=[
            pltpu.VMEM((LANES, strips * span), jnp.bfloat16),
            pltpu.VMEM((blocks, strips * span), jnp.float32),
        ],
        compiler_params=big,
        name="owner_project",
    )(params_cut, camera, slot_index, send_count)
    arrived = lax.all_to_all(message, "strip", split_axis=0, concat_axis=0, tiled=True)

    keys = tile_list.T.reshape(1, total)
    tile_cols = width // 16
    tile_num = jnp.arange(tiles, dtype=jnp.int32)
    anchor_x = tile_num % tile_cols * 16 + 8
    anchor_y = (position % per_view * (rows_strip // 16) + tile_num // tile_cols) * 16 + 8
    anchor = jnp.tile(jnp.stack([anchor_x, anchor_y]).astype(jnp.float32), (1, count))
    monomials = pixel_powers()
    powers = np.zeros((32, 256), np.float32)
    for piece in range(3):
        powers[8 * piece : 8 * piece + 6] = monomials
    moments = np.zeros((512, LANES), np.float32)
    moments[0:256, 3:9] = monomials.T
    moments[256:512, 3:9] = monomials.T
    rendered, feet, place, alpha, clear, columns = pl.pallas_call(
        functools.partial(blend_kernel, parts, tiles, chunk),
        out_shape=(
            shaped(3, tiles, 256),
            shaped(5, total),
            shaped(2, total, dtype=jnp.int32),
            shaped(total, 256),
            shaped(total, 256),
            shaped(total, 32),
        ),
        in_specs=space(vmem, vmem, vmem, vmem),
        out_specs=tuple(space(vmem, vmem, vmem, vmem, vmem, vmem)),
        scratch_shapes=[pltpu.VMEM((strips * rows, 3 * LANES), jnp.bfloat16)],
        compiler_params=big,
        name="blend",
    )(arrived, keys, anchor, jnp.asarray(powers, jnp.bfloat16))

    depth = 10
    high_rows = round_up(rows_strip + 2 * depth, 8)
    centres = round_up(rows_strip + depth, 8)
    step = position % per_view
    top = step != 0
    bottom = step != per_view - 1
    ahead = [(i, (i + 1) % strips) for i in range(strips)]
    behind = [((i + 1) % strips, i) for i in range(strips)]

    def with_halo(image):
        above = lax.ppermute(image[:, rows_strip - depth :, :], "strip", ahead)
        below = lax.ppermute(image[:, :depth, :], "strip", behind)
        fill = jnp.zeros((3, high_rows - rows_strip - 2 * depth, width), jnp.float32)
        return jnp.concatenate(
            [jnp.where(top, above, 0.0), image, jnp.where(bottom, below, 0.0), fill], axis=1
        )

    strip_rows = rows_strip // 16
    image = rendered.reshape(3, strip_rows, tile_cols, 16, 16)
    image = image.transpose(0, 1, 3, 2, 4).reshape(3, rows_strip, width)
    centre = jnp.arange(centres, dtype=jnp.int32)[:, None]
    inside = ((centre >= 5) | top) & ((centre < rows_strip + 5) | bottom)
    inside = (inside & (centre < rows_strip + depth)).astype(jnp.float32)
    render_grad = pl.pallas_call(
        loss_kernel,
        out_shape=shaped(3, rows_strip, width),
        compiler_params=big,
        name="window_loss",
    )(
        with_halo(image),
        with_halo(target),
        inside,
        band(rows_strip + depth, centres, high_rows, 0),
        band(rows_strip, rows_strip, centres, 0),
        band(width, width, width, -5),
    )
    cotangent = render_grad.reshape(3, strip_rows, 16, tile_cols, 16)
    cotangent = cotangent.transpose(0, 1, 3, 2, 4).reshape(3, tiles, 256)
    slopes = pl.pallas_call(
        functools.partial(return_kernel, strips, rows, parts, tiles, chunk),
        out_shape=shaped(strips * rows, LANES),
        scratch_shapes=[
            pltpu.VMEM((total, 256), jnp.float32),
            pltpu.VMEM((total, LANES), jnp.float32),
        ],
        compiler_params=big,
        name="blend_pull",
    )(cotangent, feet, place, alpha, clear, columns, jnp.asarray(moments, jnp.bfloat16))
    returned = lax.all_to_all(
        slopes.reshape(strips, rows, LANES), "strip", split_axis=0, concat_axis=0, tiled=True
    )
    grads = pl.pallas_call(
        functools.partial(gather_kernel, geometry),
        out_shape=shaped(59, blocks, LANES),
        in_specs=space(vmem, smem, vmem, vmem, vmem),
        scratch_shapes=[pltpu.VMEM((FEET * blocks, LANES), jnp.float32)],
        compiler_params=big,
        name="owner_pull",
    )(params_cut, camera, slot_index, view, returned)
    return grads.reshape(59, local)


def solution(mesh):
    return jax.shard_map(
        per_device,
        mesh=mesh,
        in_specs=(
            P(None, "strip"),
            P(),
            P("strip", None),
            P("strip"),
            P("strip", None),
            P(None, "strip", None),
        ),
        out_specs=P(None, "strip"),
        check_vma=False,
    )
```

```python
import functools
import math

import jax
import jax.numpy as jnp
import numpy as np
from jax import lax
from jax.experimental import pallas as pl
from jax.experimental.pallas import tpu as pltpu
from jax.sharding import PartitionSpec as P

VIEWS = 4
FEET = 9
LANES = 128
LOG2E = math.log2(math.e)
NT = (((1,), (1,)), ((), ()))

exact_dot = lax.Precision.HIGHEST
harmonic_zero = 0.28209479177387814
harmonic_one = 0.4886025119029199
harmonic_two = (
    1.0925484305920792,
    -1.0925484305920792,
    0.31539156525252005,
    -1.0925484305920792,
    0.5462742152960396,
)
harmonic_three = (
    -0.5900435899266435,
    2.890611442640554,
    -0.4570457994644658,
    0.3731763325901154,
    -0.4570457994644658,
    1.445305721320277,
    -0.5900435899266435,
)
light_term = 0.0001
contrast_term = 0.0009


def harmonics(along_x, along_y, along_z):
    square_x = along_x * along_x
    square_y = along_y * along_y
    square_z = along_z * along_z
    return [
        harmonic_zero + 0.0 * along_x,
        -harmonic_one * along_y,
        harmonic_one * along_z,
        -harmonic_one * along_x,
        harmonic_two[0] * along_x * along_y,
        harmonic_two[1] * along_y * along_z,
        harmonic_two[2] * (2.0 * square_z - square_x - square_y),
        harmonic_two[3] * along_x * along_z,
        harmonic_two[4] * (square_x - square_y),
        harmonic_three[0] * along_y * (3.0 * square_x - square_y),
        harmonic_three[1] * along_x * along_y * along_z,
        harmonic_three[2] * along_y * (4.0 * square_z - square_x - square_y),
        harmonic_three[3] * along_z * (2.0 * square_z - 3.0 * square_x - 3.0 * square_y),
        harmonic_three[4] * along_x * (4.0 * square_z - square_x - square_y),
        harmonic_three[5] * along_z * (square_x - square_y),
        harmonic_three[6] * along_x * (square_x - 3.0 * square_y),
    ]


def project(params, camera, focal, centre_x, centre_y):
    rotation = [[camera[3 * row + col] for col in range(3)] for row in range(3)]
    mean = [params[axis] for axis in range(3)]
    placed = [
        rotation[row][0] * mean[0]
        + rotation[row][1] * mean[1]
        + rotation[row][2] * mean[2]
        + camera[9 + row]
        for row in range(3)
    ]
    depth = placed[2]
    inverse = 1.0 / depth
    screen_x = focal * placed[0] * inverse + centre_x
    screen_y = focal * placed[1] * inverse + centre_y
    quaternion = params[6:10]
    shrink = lax.rsqrt(sum(part * part for part in quaternion))
    real, imag_x, imag_y, imag_z = [part * shrink for part in quaternion]
    turn = [
        [
            1.0 - 2.0 * (imag_y * imag_y + imag_z * imag_z),
            2.0 * (imag_x * imag_y - real * imag_z),
            2.0 * (imag_x * imag_z + real * imag_y),
        ],
        [
            2.0 * (imag_x * imag_y + real * imag_z),
            1.0 - 2.0 * (imag_x * imag_x + imag_z * imag_z),
            2.0 * (imag_y * imag_z - real * imag_x),
        ],
        [
            2.0 * (imag_x * imag_z - real * imag_y),
            2.0 * (imag_y * imag_z + real * imag_x),
            1.0 - 2.0 * (imag_x * imag_x + imag_y * imag_y),
        ],
    ]
    scales = [jnp.exp(part) for part in params[3:6]]
    jacobian = [
        [focal * inverse, None, -focal * placed[0] * inverse * inverse],
        [None, focal * inverse, -focal * placed[1] * inverse * inverse],
    ]
    facing = [
        [
            jacobian[row][row] * rotation[row][col]
            + jacobian[row][2] * rotation[2][col]
            for col in range(3)
        ]
        for row in range(2)
    ]
    stretch = [
        [
            (
                facing[row][0] * turn[0][col]
                + facing[row][1] * turn[1][col]
                + facing[row][2] * turn[2][col]
            )
            * scales[col]
            for col in range(3)
        ]
        for row in range(2)
    ]
    cov_xx = (
        stretch[0][0] * stretch[0][0]
        + stretch[0][1] * stretch[0][1]
        + stretch[0][2] * stretch[0][2]
        + 0.3
    )
    cov_xy = (
        stretch[0][0] * stretch[1][0]
        + stretch[0][1] * stretch[1][1]
        + stretch[0][2] * stretch[1][2]
    )
    cov_yy = (
        stretch[1][0] * stretch[1][0]
        + stretch[1][1] * stretch[1][1]
        + stretch[1][2] * stretch[1][2]
        + 0.3
    )
    determinant = cov_xx * cov_yy - cov_xy * cov_xy
    safe = [placed[0], placed[1], depth]
    length = jnp.sqrt(safe[0] * safe[0] + safe[1] * safe[1] + safe[2] * safe[2])
    heading = [
        (rotation[0][col] * safe[0] + rotation[1][col] * safe[1] + rotation[2][col] * safe[2])
        / length
        for col in range(3)
    ]
    basis = harmonics(heading[0], heading[1], heading[2])
    colour = [
        0.5 + sum(basis[k] * params[11 + 3 * k + channel] for k in range(16)) for channel in range(3)
    ]
    log_opacity = -jnp.log1p(jnp.exp(-params[10]))
    return [
        screen_x,
        screen_y,
        cov_yy / determinant,
        -cov_xy / determinant,
        cov_xx / determinant,
        colour[0],
        colour[1],
        colour[2],
        log_opacity,
    ]


def similarity(mean_x, mean_y, power_x, power_y, cross):
    var_x = power_x - mean_x * mean_x
    var_y = power_y - mean_y * mean_y
    covar = cross - mean_x * mean_y
    upper = (2.0 * mean_x * mean_y + light_term) * (2.0 * covar + contrast_term)
    lower = (mean_x * mean_x + mean_y * mean_y + light_term) * (var_x + var_y + contrast_term)
    return upper / lower


def iota(shape, dim):
    return lax.broadcasted_iota(jnp.int32, shape, dim)


def split_three(values):
    high = values.astype(jnp.bfloat16)
    rest = values - high.astype(jnp.float32)
    middle = rest.astype(jnp.bfloat16)
    low = (rest - middle.astype(jnp.float32)).astype(jnp.bfloat16)
    return high, middle, low


def split_two(values):
    high = values.astype(jnp.bfloat16)
    return high, (values - high.astype(jnp.float32)).astype(jnp.bfloat16)


def one_hot(row, size, dtype=jnp.float32):
    hit = iota((size, row.shape[1]), 0) == row
    return jnp.where(hit, 1.0, 0.0).astype(dtype)


def pick_camera(view, camera_ref):
    picked = []
    for entry in range(12):
        value = jnp.full(view.shape, camera_ref[0, entry], jnp.float32)
        for number in range(1, VIEWS):
            value = jnp.where(view == float(number), camera_ref[number, entry], value)
        picked.append(value)
    return picked


def owner_kernel(
    geometry, offset, per_view, params_ref, camera_ref, index_ref, count_ref,
    message_ref, view_ref, low_ref, owner_ref
):
    strips = message_ref.shape[0]
    blocks = params_ref.shape[1]
    slots = index_ref.shape[1]
    span = slots // strips
    parts = span // LANES

    @pl.loop(0, strips)
    def _(strip):
        here = pl.ds(pl.multiple_of(strip * span, LANES), span)
        index = index_ref[:, here]
        low_ref[:, here] = one_hot(index & 127, LANES, jnp.bfloat16)
        view = (lax.rem(strip + offset, strips) // per_view).astype(jnp.float32)
        live = iota((1, span), 1) < count_ref[strip]
        mark = jnp.where(live, view, 0.0)
        owner_ref[:, here] = one_hot(index >> 7, blocks) * mark

    view = lax.dot_general(
        owner_ref[...].astype(jnp.bfloat16), low_ref[...], NT, preferred_element_type=jnp.float32
    )
    view_ref[...] = view
    camera = pick_camera(view, camera_ref)
    feet = project([params_ref[entry] for entry in range(59)], camera, *geometry)
    high, middle, third = split_three(jnp.concatenate(feet, axis=0))
    packed = jnp.concatenate([high, middle], axis=1)
    third = third[0 : 2 * blocks]

    @pl.loop(0, strips)
    def _(strip):
        here = pl.ds(pl.multiple_of(strip * span, LANES), span)
        low = low_ref[:, here]
        found = jnp.dot(
            packed, jnp.concatenate([low, low], axis=0), preferred_element_type=jnp.float32
        ).reshape(FEET, blocks, span)
        fine = jnp.dot(third, low, preferred_element_type=jnp.float32).reshape(2, blocks, span)
        found = jnp.concatenate([found[0:2] + fine, found[2:]], axis=0)
        high = one_hot(index_ref[:, here] >> 7, blocks)
        chosen = jnp.sum(found * high[None], axis=1)
        for part in range(parts):
            message_ref[strip, part * FEET : (part + 1) * FEET, :] = chosen[
                :, part * LANES : (part + 1) * LANES
            ]
        message_ref[strip, parts * FEET : parts * FEET + 1, :] = jnp.full(
            (1, LANES), count_ref[strip].astype(jnp.float32)
        )


def source_hits(starts, ends, keys):
    return jnp.where((keys >= starts) & (keys < ends), 1.0, 0.0)


def blend_kernel(
    parts, tiles, chunk, arrived_ref, keys_ref, anchor_ref, powers_ref,
    rendered_ref, feet_ref, place_ref, columns_ref, alpha_ref, packed_ref, third_ref
):
    strips, rows, _ = arrived_ref.shape
    total = keys_ref.shape[1]
    counts = arrived_ref[:, parts * FEET, :]
    order = iota((strips, strips), 0) >= iota((strips, strips), 1)
    ends = jnp.dot(
        jnp.where(order, 1.0, 0.0), counts, precision=exact_dot, preferred_element_type=jnp.float32
    )
    starts = ends - counts
    ends = ends[:, 0:1]
    starts = starts[:, 0:1]
    span = parts * LANES
    for foot in range(FEET):
        block = jnp.concatenate(
            [arrived_ref[:, part * FEET + foot, :] for part in range(parts)], axis=1
        )
        high, middle, third = split_three(block)
        here = slice(foot * strips, (foot + 1) * strips)
        packed_ref[here, 0:span] = high
        packed_ref[here, span : 2 * span] = middle
        if foot < 2:
            third_ref[here, :] = third
    powers = powers_ref[...]

    @pl.loop(0, total // chunk)
    def _(step):
        here = pl.ds(pl.multiple_of(step * chunk, LANES), chunk)
        keys = keys_ref[:, here].astype(jnp.float32)
        hits = source_hits(starts, ends, keys)
        slot = (keys - jnp.sum(hits * starts, axis=0, keepdims=True)).astype(jnp.int32)
        low = one_hot(slot, span, jnp.bfloat16)
        found = jnp.dot(
            packed_ref[...],
            jnp.concatenate([low, low], axis=0),
            preferred_element_type=jnp.float32,
        ).reshape(FEET, strips, chunk)
        fine = jnp.dot(
            third_ref[...], low, preferred_element_type=jnp.float32
        ).reshape(2, strips, chunk)
        found = jnp.concatenate([found[0:2] + fine, found[2:]], axis=0)
        feet = jnp.sum(found * hits[None], axis=1)
        source = jnp.sum(hits * iota(hits.shape, 0).astype(jnp.float32), axis=0, keepdims=True)
        place_ref[0:1, here] = source.astype(jnp.int32)
        place_ref[1:2, here] = slot
        row = [feet[entry : entry + 1] for entry in range(FEET)]
        off_x = row[0] - anchor_ref[0:1, here]
        off_y = row[1] - anchor_ref[1:2, here]
        conic_a, conic_b, conic_c = row[2], row[3], row[4]
        feet_ref[:, here] = jnp.concatenate([off_x, off_y, conic_a, conic_b, conic_c], axis=0)
        terms = jnp.concatenate(
            [
                LOG2E
                * (
                    row[8]
                    - 0.5 * (conic_a * off_x * off_x + conic_c * off_y * off_y)
                    - conic_b * off_x * off_y
                ),
                LOG2E * (conic_a * off_x + conic_b * off_y),
                LOG2E * (conic_c * off_y + conic_b * off_x),
                (-0.5 * LOG2E) * conic_a,
                -LOG2E * conic_b,
                (-0.5 * LOG2E) * conic_c,
                jnp.zeros((2, chunk), jnp.float32),
            ],
            axis=0,
        )
        pieces = [piece.astype(jnp.float32) for piece in split_three(terms)]
        colours = jnp.concatenate(row[5:8] + [jnp.zeros((5, chunk), jnp.float32)], axis=0)
        columns = jnp.transpose(jnp.concatenate(pieces + [colours], axis=0))
        columns_ref[here, :] = columns
        power = jnp.dot(columns.astype(jnp.bfloat16), powers, preferred_element_type=jnp.float32)
        alpha_ref[here, :] = jnp.exp2(power)

    def forward(entry, carry):
        clear, red, green, blue = carry
        here = pl.ds(pl.multiple_of(entry * tiles, 8), tiles)
        weight = alpha_ref[here, :] * clear
        tint = columns_ref[here, :]
        return (
            clear - weight,
            red + tint[:, 24:25] * weight,
            green + tint[:, 25:26] * weight,
            blue + tint[:, 26:27] * weight,
        )

    nothing = jnp.zeros((tiles, 256), jnp.float32)
    _, red, green, blue = lax.fori_loop(
        0, total // tiles, forward, (nothing + 1.0, nothing, nothing, nothing), unroll=2
    )
    rendered_ref[0] = red
    rendered_ref[1] = green
    rendered_ref[2] = blue


def loss_kernel(whole_ref, truth_ref, inside_ref, down_ref, back_ref, across_ref, grad_ref):
    rows = grad_ref.shape[1]
    centres = down_ref.shape[0]
    fields = []
    for channel in range(3):
        seen = whole_ref[channel]
        truth = truth_ref[channel]
        fields += [seen, truth, seen * seen, truth * truth, seen * truth]

    def smooth(matrix, items):
        stacked = jnp.concatenate(
            [
                jnp.dot(matrix, item, precision=exact_dot, preferred_element_type=jnp.float32)
                for item in items
            ],
            axis=0,
        )
        return jnp.dot(
            stacked, across_ref[...], precision=exact_dot, preferred_element_type=jnp.float32
        )

    smoothed = smooth(down_ref[...], fields)
    inside = inside_ref[...]
    partials = []
    for channel in range(3):
        mean_x, mean_y, power_x, power_y, cross = [
            smoothed[(5 * channel + item) * centres : (5 * channel + item + 1) * centres]
            for item in range(5)
        ]
        value, pull = jax.vjp(
            lambda first, second, third: similarity(first, mean_y, second, power_y, third),
            mean_x,
            power_x,
            cross,
        )
        partials += [
            jnp.where(inside > 0.0, part, 0.0) for part in pull(jnp.full_like(value, -1.0))
        ]
    spread = smooth(back_ref[...], partials)
    depth = 10
    for channel in range(3):
        first, second, third = [
            spread[(3 * channel + item) * rows : (3 * channel + item + 1) * rows]
            for item in range(3)
        ]
        seen = whole_ref[channel][depth : depth + rows]
        truth = truth_ref[channel][depth : depth + rows]
        grad_ref[channel] = first + 2.0 * seen * second + truth * third


def pull_kernel(
    parts, tiles, chunk, grad_ref, feet_ref, place_ref, columns_ref, powers_ref,
    moments_ref, change_ref, tints_ref, alpha_ref, pass_ref
):
    total = feet_ref.shape[1]
    entries = total // tiles
    grads = [grad_ref[channel] for channel in range(3)]
    powers = powers_ref[...]

    @pl.loop(0, total // chunk)
    def _(step):
        here = pl.ds(pl.multiple_of(step * chunk, LANES), chunk)
        alpha_ref[here, :] = jnp.exp2(
            jnp.dot(
                columns_ref[here, :].astype(jnp.bfloat16),
                powers,
                preferred_element_type=jnp.float32,
            )
        )

    def forward(entry, clear):
        here = pl.ds(pl.multiple_of(entry * tiles, 8), tiles)
        pass_ref[here, :] = clear
        return clear - alpha_ref[here, :] * clear

    lax.fori_loop(0, entries, forward, jnp.ones((tiles, 256), jnp.float32), unroll=4)
    lane = iota((tiles, LANES), 1)

    def backward(step, behind):
        entry = entries - 1 - step
        here = pl.ds(pl.multiple_of(entry * tiles, 8), tiles)
        alpha = alpha_ref[here, :]
        clear = pass_ref[here, :]
        tint = columns_ref[here, :]
        shade = (
            grads[0] * tint[:, 24:25] + grads[1] * tint[:, 25:26] + grads[2] * tint[:, 26:27]
        )
        excess = shade - behind
        weight = alpha * clear
        change_ref[here, :] = weight * excess
        sums = [jnp.sum(weight * grad, axis=1, keepdims=True) for grad in grads]
        tints_ref[here, :] = jnp.where(
            lane == 0, sums[0], jnp.where(lane == 1, sums[1], jnp.where(lane == 2, sums[2], 0.0))
        )
        return behind + alpha * excess

    lax.fori_loop(
        0, entries, backward, jnp.zeros((tiles, 256), jnp.float32), unroll=2
    )
    moments = moments_ref[...]
    return moments, total


def scatter_steps(strips, rows, parts, chunk, refs, moments, total):
    feet_ref, place_ref, message_ref, change_ref, tints_ref, sum_ref = refs
    sum_ref[...] = jnp.zeros_like(sum_ref)

    @pl.loop(0, total // chunk)
    def _(step):
        here = pl.ds(pl.multiple_of(step * chunk, LANES), chunk)
        high, low = split_two(change_ref[here, :])
        sums = tints_ref[here, :] + jnp.dot(
            jnp.concatenate([high, low], axis=1), moments, preferred_element_type=jnp.float32
        )
        lines = jnp.transpose(sums)
        plain, by_x, by_y, by_xx, by_xy, by_yy = [lines[item : item + 1] for item in range(3, 9)]
        feet = feet_ref[:, here]
        off_x, off_y, conic_a, conic_b, conic_c = [feet[item : item + 1] for item in range(5)]
        far_x = by_x - off_x * plain
        far_y = by_y - off_y * plain
        far_xx = by_xx - 2.0 * off_x * by_x + off_x * off_x * plain
        far_yy = by_yy - 2.0 * off_y * by_y + off_y * off_y * plain
        far_xy = by_xy - off_x * by_y - off_y * by_x + off_x * off_y * plain
        slopes = jnp.concatenate(
            [
                conic_a * far_x + conic_b * far_y,
                conic_c * far_y + conic_b * far_x,
                -0.5 * far_xx,
                -far_xy,
                -0.5 * far_yy,
                lines[0:3],
                plain,
            ],
            axis=0,
        )
        source = place_ref[0:1, here]
        slot = place_ref[1:2, here]
        first = slopes.astype(jnp.bfloat16).astype(jnp.float32)
        hits = one_hot(source, strips)[None]
        spread = jnp.concatenate(
            [
                (hits * piece[:, None, :]).reshape(FEET * strips, chunk).astype(jnp.bfloat16)
                for piece in (first, slopes - first)
            ],
            axis=1,
        )
        lows = one_hot(slot, parts * LANES, jnp.bfloat16)
        sum_ref[...] += lax.dot_general(
            spread,
            jnp.concatenate([lows, lows], axis=1),
            NT,
            preferred_element_type=jnp.float32,
        )

    for foot in range(FEET):
        for part in range(parts):
            message_ref[:, part * FEET + foot, :] = sum_ref[
                foot * strips : (foot + 1) * strips, part * LANES : (part + 1) * LANES
            ]


def return_kernel(
    strips, rows, parts, tiles, chunk, grad_ref, feet_ref, place_ref, columns_ref, powers_ref,
    moments_ref, message_ref, change_ref, tints_ref, sum_ref, alpha_ref, pass_ref
):
    moments, total = pull_kernel(
        parts, tiles, chunk, grad_ref, feet_ref, place_ref, columns_ref, powers_ref,
        moments_ref, change_ref, tints_ref, alpha_ref, pass_ref
    )
    refs = (feet_ref, place_ref, message_ref, change_ref, tints_ref, sum_ref)
    scatter_steps(strips, rows, parts, chunk, refs, moments, total)


def gather_kernel(
    geometry, params_ref, camera_ref, index_ref, view_ref, returned_ref, out_ref, sum_ref
):
    strips = returned_ref.shape[0]
    blocks = params_ref.shape[1]
    span = index_ref.shape[1] // strips
    parts = span // LANES
    sum_ref[...] = jnp.zeros_like(sum_ref)

    @pl.loop(0, strips)
    def _(strip):
        here = pl.ds(pl.multiple_of(strip * span, LANES), span)
        index = index_ref[:, here]
        low = one_hot(index & 127, LANES, jnp.bfloat16)
        high = one_hot(index >> 7, blocks)[None]
        block = returned_ref[strip]
        slopes = jnp.concatenate(
            [block[part * FEET : (part + 1) * FEET] for part in range(parts)], axis=1
        )
        first = slopes.astype(jnp.bfloat16).astype(jnp.float32)
        spread = jnp.concatenate(
            [
                (high * piece[:, None, :]).reshape(FEET * blocks, span).astype(jnp.bfloat16)
                for piece in (first, slopes - first)
            ],
            axis=1,
        )
        sum_ref[...] += lax.dot_general(
            spread, jnp.concatenate([low, low], axis=1), NT, preferred_element_type=jnp.float32
        )

    camera = pick_camera(view_ref[...], camera_ref)
    ignored, pull = jax.vjp(
        lambda values: project(values, camera, *geometry),
        [params_ref[entry] for entry in range(59)],
    )
    slopes = [sum_ref[entry * blocks : (entry + 1) * blocks, :] for entry in range(FEET)]
    for entry, slope in enumerate(pull(slopes)[0]):
        out_ref[entry] = slope


def window_weights():
    offsets = np.arange(11, dtype=np.float64) - 5.0
    raw = np.exp(-offsets * offsets / 4.5)
    return raw / raw.sum()


def band(out_rows, out_pad, in_pad, shift):
    weights = window_weights()
    matrix = np.zeros((out_pad, in_pad), np.float32)
    for row in range(out_rows):
        for tap in range(11):
            column = row + tap + shift
            if 0 <= column < in_pad:
                matrix[row, column] = weights[tap]
    return matrix


def pixel_powers():
    pixel = np.arange(256)
    along_x = pixel % 16 - 7.5
    along_y = pixel // 16 - 7.5
    return np.stack(
        [
            np.ones(256),
            along_x,
            along_y,
            along_x * along_x,
            along_x * along_y,
            along_y * along_y,
        ]
    )


def round_up(value, step):
    return -(-value // step) * step


def per_device(params, camera, send_index, send_count, tile_list, target):
    strips = lax.axis_size("strip")
    index = lax.axis_index("strip")
    per_view = strips // VIEWS
    offset = per_view // 2
    position = (index + offset) % strips
    rows_strip = target.shape[1]
    width = target.shape[2]
    view_rows = rows_strip * per_view
    focal = 0.5 * width
    geometry = (focal, 0.5 * width, 0.5 * view_rows)
    tiles, count = tile_list.shape
    total = tiles * count
    chunk = math.gcd(512, total)
    capacity = send_index.shape[1]
    parts = -(-capacity // LANES)
    span = parts * LANES
    rows = round_up(parts * FEET + 1, 16)
    local = params.shape[1]
    blocks = local // LANES
    vmem = pltpu.MemorySpace.VMEM
    smem = pltpu.MemorySpace.SMEM
    big = pltpu.CompilerParams(vmem_limit_bytes=56 * 1024 * 1024)

    def space(*kinds):
        return [pl.BlockSpec(memory_space=kind) for kind in kinds]

    def shaped(*shape, dtype=jnp.float32):
        return jax.ShapeDtypeStruct(shape, dtype)

    params_cut = params.reshape(59, blocks, LANES)
    slot_index = jnp.pad(send_index, ((0, 0), (0, span - capacity))).reshape(1, strips * span)
    message, view = pl.pallas_call(
        functools.partial(owner_kernel, geometry, offset, per_view),
        out_shape=(shaped(strips, rows, LANES), shaped(blocks, LANES)),
        in_specs=space(vmem, smem, vmem, smem),
        out_specs=tuple(space(vmem, vmem)),
        scratch_shapes=[
            pltpu.VMEM((LANES, strips * span), jnp.bfloat16),
            pltpu.VMEM((blocks, strips * span), jnp.float32),
        ],
        compiler_params=big,
        name="owner_project",
    )(params_cut, camera, slot_index, send_count)
    arrived = lax.all_to_all(message, "strip", split_axis=0, concat_axis=0, tiled=True)

    keys = tile_list.T.reshape(1, total)
    tile_cols = width // 16
    tile_num = jnp.arange(tiles, dtype=jnp.int32)
    anchor_x = tile_num % tile_cols * 16 + 8
    anchor_y = (position % per_view * (rows_strip // 16) + tile_num // tile_cols) * 16 + 8
    anchor = jnp.tile(jnp.stack([anchor_x, anchor_y]).astype(jnp.float32), (1, count))
    monomials = pixel_powers()
    powers = np.zeros((32, 256), np.float32)
    for piece in range(3):
        powers[8 * piece : 8 * piece + 6] = monomials
    moments = np.zeros((512, LANES), np.float32)
    moments[0:256, 3:9] = monomials.T
    moments[256:512, 3:9] = monomials.T
    rendered, feet, place, columns = pl.pallas_call(
        functools.partial(blend_kernel, parts, tiles, chunk),
        out_shape=(
            shaped(3, tiles, 256),
            shaped(5, total),
            shaped(2, total, dtype=jnp.int32),
            shaped(total, 32),
        ),
        in_specs=space(vmem, vmem, vmem, vmem),
        out_specs=tuple(space(vmem, vmem, vmem, vmem)),
        scratch_shapes=[
            pltpu.VMEM((total, 256), jnp.float32),
            pltpu.VMEM((FEET * strips, 2 * span), jnp.bfloat16),
            pltpu.VMEM((2 * strips, span), jnp.bfloat16),
        ],
        compiler_params=big,
        name="blend",
    )(arrived, keys, anchor, jnp.asarray(powers, jnp.bfloat16))

    depth = 10
    high_rows = round_up(rows_strip + 2 * depth, 8)
    centres = round_up(rows_strip + depth, 8)
    step = position % per_view
    top = step != 0
    bottom = step != per_view - 1
    ahead = [(i, (i + 1) % strips) for i in range(strips)]
    behind = [((i + 1) % strips, i) for i in range(strips)]

    def with_halo(image):
        above = lax.ppermute(image[:, rows_strip - depth :, :], "strip", ahead)
        below = lax.ppermute(image[:, :depth, :], "strip", behind)
        fill = jnp.zeros((3, high_rows - rows_strip - 2 * depth, width), jnp.float32)
        return jnp.concatenate(
            [jnp.where(top, above, 0.0), image, jnp.where(bottom, below, 0.0), fill], axis=1
        )

    strip_rows = rows_strip // 16
    image = rendered.reshape(3, strip_rows, tile_cols, 16, 16)
    image = image.transpose(0, 1, 3, 2, 4).reshape(3, rows_strip, width)
    centre = jnp.arange(centres, dtype=jnp.int32)[:, None]
    inside = ((centre >= 5) | top) & ((centre < rows_strip + 5) | bottom)
    inside = (inside & (centre < rows_strip + depth)).astype(jnp.float32)
    render_grad = pl.pallas_call(
        loss_kernel,
        out_shape=shaped(3, rows_strip, width),
        compiler_params=big,
        name="window_loss",
    )(
        with_halo(image),
        with_halo(target),
        inside,
        band(rows_strip + depth, centres, high_rows, 0),
        band(rows_strip, rows_strip, centres, 0),
        band(width, width, width, -5),
    )
    cotangent = render_grad.reshape(3, strip_rows, 16, tile_cols, 16)
    cotangent = cotangent.transpose(0, 1, 3, 2, 4).reshape(3, tiles, 256)
    slopes = pl.pallas_call(
        functools.partial(return_kernel, strips, rows, parts, tiles, chunk),
        out_shape=shaped(strips, rows, LANES),
        scratch_shapes=[
            pltpu.VMEM((total, 256), jnp.float32),
            pltpu.VMEM((total, LANES), jnp.float32),
            pltpu.VMEM((FEET * strips, span), jnp.float32),
            pltpu.VMEM((total, 256), jnp.float32),
            pltpu.VMEM((total, 256), jnp.float32),
        ],
        compiler_params=big,
        name="blend_pull",
    )(
        cotangent,
        feet,
        place,
        columns,
        jnp.asarray(powers, jnp.bfloat16),
        jnp.asarray(moments, jnp.bfloat16),
    )
    returned = lax.all_to_all(
        slopes, "strip", split_axis=0, concat_axis=0, tiled=True
    )
    grads = pl.pallas_call(
        functools.partial(gather_kernel, geometry),
        out_shape=shaped(59, blocks, LANES),
        in_specs=space(vmem, smem, vmem, vmem, vmem),
        scratch_shapes=[pltpu.VMEM((FEET * blocks, LANES), jnp.float32)],
        compiler_params=big,
        name="owner_pull",
    )(params_cut, camera, slot_index, view, returned)
    return grads.reshape(59, local)


def solution(mesh):
    return jax.shard_map(
        per_device,
        mesh=mesh,
        in_specs=(
            P(None, "strip"),
            P(),
            P("strip", None),
            P("strip"),
            P("strip", None),
            P(None, "strip", None),
        ),
        out_specs=P(None, "strip"),
        check_vma=False,
    )
```
